128 devices in a mesh: grp: 8 (over x, core), seq: 16 (over z, y).
Axes of the slice: x: 4, y: 4, z: 4, core: 2. Of those that a mesh axis runs over, the one named last changes fastest.
Arguments:
- queries: bfloat16 [32768, 2048], P(('grp', 'seq')), may hold values from -11 to 11
- keys: bfloat16 [32768, 2048], P(('grp', 'seq')), may hold values from -11 to 11
- values: bfloat16 [32768, 2048], P(('grp', 'seq')), may hold values from -6 to 6
- out_grad: bfloat16 [32768, 2048], P(('grp', 'seq')), may hold values from -6 to 6
- doc_ids: int32 [32768], P(('grp', 'seq')), may hold values from 0 to 47, never falling along the last dimension, each value on 1 to 1024 neighbouring positions
Outputs:
- attn_out: bfloat16 [32768, 2048], P(('grp', 'seq'))
- query_grad: bfloat16 [32768, 2048], P(('grp', 'seq'))
- key_grad: bfloat16 [32768, 2048], P(('grp', 'seq'))
- value_grad: bfloat16 [32768, 2048], P(('grp', 'seq'))
The draws below stay inside these ranges and needn't reach their ends.
Inputs may be any that keep to these rules, and one draw needn't show every extreme that they name: `doc_ids`: document ids never fall along the stream; each document holds 1 to 1024 patches, and one holds exactly 1024.
All inputs are finite; a program needn't handle non-finite values.
Results may differ from the reference program's by a relative error of at most 0.028.
Values may be sent and summed in bfloat16 or wider, within the bound.
No kernel may reach another device: no remote copies, remote signals or barrier semaphores. Data moves between devices by JAX's collectives and lax.ppermute only.
A program may use at most 128 MiB of HBM per device.

```python
import math
import jax
import jax.numpy as jnp
import numpy as np
from jax import lax

HEADS = 16
HEAD_DIM = 128
REACH = 4
PATCH_DEV = 256
FEATURES = 2048
PATCHES = 32768
DOC_MOST = 1024
DOCS = 48


def draw_queries(key, part):
    key = jax.random.fold_in(key, 1)
    return jax.random.normal(key, (PATCHES, FEATURES), jnp.float32).clip(-6.0, 6.0).astype(jnp.bfloat16)


def draw_keys(key, part):
    key = jax.random.fold_in(key, 2)
    return jax.random.normal(key, (PATCHES, FEATURES), jnp.float32).clip(-6.0, 6.0).astype(jnp.bfloat16)


def steps_of(stream_key, dims, split, least, largest):
    factor_of = 1.0
    for dim, parts in split:
        heights = jax.random.uniform(jax.random.fold_in(jax.random.fold_in(stream_key, 6), dim), (parts,), jnp.float32, least / len(split), largest / len(split))
        factor_of = factor_of * jnp.repeat(jnp.exp(heights), dims[dim] // parts).reshape((-1,) + (1,) * (len(dims) - 1 - dim))
    return factor_of


def profile(count, total, limit, slope):
    weights = [(1 << 20) // math.isqrt(rank ** slope) + 1 for rank in range(2, count + 1)]
    surplus, holding = total - limit - (count - 1), [1] * (count - 1)
    while surplus > 0:
        candidates = [i for i in range(count - 1) if holding[i] < limit]
        pool, remaining = sum([weights[i] for i in candidates]), surplus
        for i in candidates:
            addition = min(limit - holding[i], max(1, remaining * weights[i] // pool), surplus)
            holding[i] = holding[i] + addition
            surplus = surplus - addition
    return np.array([limit] + holding)


def uneven_parts(stream_key, count, total, limit, lean):
    if count == 2:
        one = jax.random.randint(stream_key, (), max(1, total - limit), min(limit, total - 1) + 1)
        return jnp.stack([one, total - one])
    lengths = jnp.asarray(profile(count, total, limit, lean), jnp.int32)
    couples = (count - 1) // 2
    giver, receiver = lengths[1:1 + 2 * couples:2], lengths[2:2 + 2 * couples:2]
    slack = jnp.minimum(giver - 1, limit - receiver)
    shifted = jax.random.randint(jax.random.fold_in(stream_key, 1), (couples,), 0, 1 << 20) % (slack + 1)
    lengths = lengths.at[1:1 + 2 * couples:2].set(giver - shifted).at[2:2 + 2 * couples:2].set(receiver + shifted)
    return lengths[jax.random.permutation(jax.random.fold_in(stream_key, 2), count)]


def centred(stream_key, shape, deviation, limit, shards=(), held_as=jnp.bfloat16):
    values = deviation * jax.random.normal(stream_key, shape, jnp.float32)
    if shards:
        values = values * steps_of(stream_key, shape, shards, -0.22, 0.18)
    return jnp.clip(values, -limit, limit).astype(held_as)


def setup_inputs(seed: int = 0) -> dict:
    key_list = jax.random.split(jax.random.key(seed), 6)
    queries = draw_queries(jax.random.fold_in(key_list[5], 71), 0)
    keys = draw_keys(jax.random.fold_in(key_list[5], 71), 0)
    values = centred(key_list[2], (PATCHES, FEATURES), 1.0, 6.0, ((0, 128),))
    out_grad = centred(key_list[3], (PATCHES, FEATURES), 1.0, 6.0, ((0, 128),))
    doc_ids = jnp.searchsorted(jnp.cumsum(uneven_parts(key_list[4], DOCS, PATCHES, DOC_MOST, 2)), jnp.arange(PATCHES), side="right").astype(jnp.int32)
    return dict(queries=queries, keys=keys, values=values, out_grad=out_grad, doc_ids=doc_ids)


def reference(queries, keys, values, out_grad, doc_ids):
    rows = PATCH_DEV
    margin = REACH * rows
    window = (REACH + 1) * rows
    blocks = PATCHES // rows
    scale = 1.0 / math.sqrt(HEAD_DIM)
    q_heads = queries.astype(jnp.float32).reshape(PATCHES, HEADS, HEAD_DIM)
    g_heads = out_grad.astype(jnp.float32).reshape(PATCHES, HEADS, HEAD_DIM)
    front = jnp.zeros((margin, HEADS, HEAD_DIM), jnp.float32)
    k_padded = jnp.concatenate([front, keys.astype(jnp.float32).reshape(PATCHES, HEADS, HEAD_DIM)], axis=0)
    v_padded = jnp.concatenate([front, values.astype(jnp.float32).reshape(PATCHES, HEADS, HEAD_DIM)], axis=0)
    d_padded = jnp.concatenate([jnp.full((margin,), -1, jnp.int32), doc_ids.astype(jnp.int32)], axis=0)

    def step(carry, index):
        key_total, value_total = carry
        start = (index * rows).astype(jnp.int32)
        q_block = lax.dynamic_slice_in_dim(q_heads, start, rows, 0)
        g_block = lax.dynamic_slice_in_dim(g_heads, start, rows, 0)
        q_docs = lax.dynamic_slice_in_dim(doc_ids, start, rows, 0)
        k_block = lax.dynamic_slice_in_dim(k_padded, start, window, 0)
        v_block = lax.dynamic_slice_in_dim(v_padded, start, window, 0)
        k_docs = lax.dynamic_slice_in_dim(d_padded, start, window, 0)
        q_pos = start + jnp.arange(rows, dtype=jnp.int32)
        k_pos = start - margin + jnp.arange(window, dtype=jnp.int32)
        mask = (q_docs[:, None] == k_docs[None, :]) & (k_pos[None, :] <= q_pos[:, None])
        score = jnp.einsum('qhd,khd->hqk', q_block, k_block) * scale
        score = jnp.where(mask[None], score, -1e+30)
        top = lax.optimization_barrier(jnp.max(score, axis=-1))
        lse = top + jnp.log(lax.optimization_barrier(jnp.sum(jnp.exp(score - top[..., None]), axis=-1)))
        prob = jnp.where(mask[None], jnp.exp(score - lse[..., None]), 0.0)
        prob_low = lax.optimization_barrier(prob.astype(jnp.bfloat16)).astype(jnp.float32)
        out = jnp.einsum('hqk,khd->qhd', prob_low, v_block).astype(jnp.bfloat16)
        delta = lax.optimization_barrier(jnp.sum(g_block * out.astype(jnp.float32), axis=-1)).T
        dprob = jnp.einsum('qhd,khd->hqk', g_block, v_block)
        dscore = (prob * (dprob - delta[..., None]) * scale).astype(jnp.bfloat16)
        dscore = lax.optimization_barrier(dscore).astype(jnp.float32)
        dq = jnp.einsum('hqk,khd->qhd', dscore, k_block).astype(jnp.bfloat16)
        key_part = lax.optimization_barrier(jnp.einsum('hqk,qhd->khd', dscore, q_block).astype(jnp.bfloat16)).astype(jnp.float32)
        value_part = lax.optimization_barrier(jnp.einsum('hqk,qhd->khd', prob_low, g_block).astype(jnp.bfloat16)).astype(jnp.float32)
        key_total = lax.dynamic_update_slice_in_dim(key_total, lax.dynamic_slice_in_dim(key_total, start, window, 0) + key_part, start, 0)
        value_total = lax.dynamic_update_slice_in_dim(value_total, lax.dynamic_slice_in_dim(value_total, start, window, 0) + value_part, start, 0)
        return ((key_total, value_total), (out, dq))
    empty = jnp.zeros((PATCHES + margin, HEADS, HEAD_DIM), jnp.float32)
    (key_total, value_total), (outs, dqs) = lax.scan(step, (empty, empty), jnp.arange(blocks, dtype=jnp.int32))
    attn_out = outs.reshape(PATCHES, FEATURES)
    query_grad = dqs.reshape(PATCHES, FEATURES)
    key_grad = key_total[margin:].reshape(PATCHES, FEATURES).astype(jnp.bfloat16)
    value_grad = value_total[margin:].reshape(PATCHES, FEATURES).astype(jnp.bfloat16)
    return (attn_out, query_grad, key_grad, value_grad)
```

```python
import functools
import math

import jax
import jax.numpy as jnp
from jax import lax
from jax.experimental import pallas as pl
from jax.experimental.pallas import tpu as pltpu
from jax.sharding import PartitionSpec as P

HEADS = 16
HEAD_DIM = 128
ROWS = 256
GROUP = 4
SPAN = GROUP * ROWS
DOC_ROWS = 16
SCALE = 1.0 / math.sqrt(HEAD_DIM)
LOG2E = math.log2(math.e)
AXES = ("grp", "seq")
BF16 = jnp.bfloat16
F32 = jnp.float32
SMEM = pl.BlockSpec(memory_space=pltpu.SMEM)
VMEM = pl.BlockSpec(memory_space=pltpu.VMEM)
ANY = pl.BlockSpec(memory_space=pl.ANY)
HBM = pl.BlockSpec(memory_space=pltpu.HBM)
SMALL = pltpu.CompilerParams(vmem_limit_bytes=8 * 1024 * 1024)
WHOLE = pltpu.CompilerParams(vmem_limit_bytes=56 * 1024 * 1024)
LARGE = pltpu.CompilerParams(vmem_limit_bytes=24 * 1024 * 1024)
CHUNKS = ((0,), (1,), (2,), (3,))
IN = (
    (("k", 0), ("v", 0), ("doc", 0),),
    (("q", 0), ("g", 0), ("k", 1), ("v", 1),),
    (("q", 1), ("g", 1), ("k", 2), ("v", 2),),
    (("q", 2), ("g", 2), ("k", 3), ("v", 3), ("q", 3), ("g", 3),),
)
OUT = (
    (("o", 0), ("dq", 0), ("o", 1), ("dq", 1), ("dk", 0), ("dv", 0),),
    (("dk", 1), ("dv", 1), ("o", 2), ("dq", 2),),
    (("dk", 2), ("dv", 2), ("o", 3), ("dq", 3),),
    (("dk", 3), ("dv", 3),),
)
UNPACK = ((0, 1), (2, 3))
AFTER = (None, 0, 1, None)
RUNS = (3, 2, 1)
RESULTS = ("o", "dq", "dk", "dv")
WIDTH = HEADS // GROUP * HEAD_DIM


def shift_y(block, step):
    total = lax.axis_size(AXES)
    route = [(d, d // GROUP * GROUP + (d + step) % GROUP) for d in range(total)]
    return lax.ppermute(block, AXES, route)


def shift_group(block, step):
    total = lax.axis_size(AXES)
    route = [(d, (d + step * GROUP) % total) for d in range(total)]
    return lax.ppermute(block, AXES, route)


def run_copies(pairs, sem):
    copies = [pltpu.make_async_copy(src, dst, sem.at[n]) for n, (src, dst) in enumerate(pairs)]
    for copy in copies:
        copy.start()
    for copy in copies:
        copy.wait()


def rows_of(item):
    return DOC_ROWS if item[0] == "doc" else ROWS


def length(message):
    return sum(rows_of(item) for item in message)


def offset(message, item):
    return length(message[: message.index(item)])


def holder(messages, item):
    return next(n for n, message in enumerate(messages) if item in message)


def turned(y, s):
    return lax.rem(y + s + GROUP, GROUP)


def pack_kernel(messages, y_ref, k_ref, v_ref, q_ref, g_ref, doc_ref, *refs):
    *outs, sem = refs
    y = y_ref[0]
    source = {"k": k_ref, "v": v_ref, "q": q_ref, "g": g_ref}
    pairs = []
    for n, message in enumerate(messages):
        for s in range(GROUP):
            for item in message:
                name, h = item
                rows = outs[n * GROUP + s].at[pl.ds(offset(message, item), rows_of(item))]
                if name == "doc":
                    pairs.append((doc_ref, rows))
                    continue
                column = pl.multiple_of(turned(y, s) * WIDTH + h * HEAD_DIM, HEAD_DIM)
                pairs.append((source[name].at[:, pl.ds(column, HEAD_DIM)], rows))
    run_copies(pairs, sem)


def pack(messages, y, k, v, q, g, docs):
    pieces = pl.pallas_call(
        functools.partial(pack_kernel, messages),
        out_shape=[jax.ShapeDtypeStruct((length(message), HEAD_DIM), BF16)
                   for message in messages for _ in range(GROUP)],
        in_specs=[SMEM] + [HBM] * 5,
        out_specs=[VMEM] * (GROUP * len(messages)),
        scratch_shapes=[pltpu.SemaphoreType.DMA((GROUP * sum(map(len, messages)),))],
        compiler_params=WHOLE,
        name="pack",
    )(y, k, v, q, g, docs)
    return [pieces[n * GROUP: (n + 1) * GROUP] for n in range(len(messages))]


def order_kernel(message, items, y_ref, m0, m1, m2, m3, out, sem):
    y = y_ref[0]
    pairs = []
    for s, ref in enumerate((m0, m1, m2, m3)):
        at = turned(y, -s)
        for n, item in enumerate(items):
            size = rows_of(item)
            place = pl.multiple_of(n * SPAN + at * size, size)
            pairs.append((ref.at[pl.ds(offset(message, item), size)], out.at[pl.ds(place, size)]))
    run_copies(pairs, sem)


def order(chunk, y, arrived):
    items = [(name, h) for h in CHUNKS[chunk] for name in ("k", "v")]
    n = holder(IN, items[0])
    total = len(items) * SPAN
    if chunk == 0:
        items.append(("doc", 0))
        total += GROUP * DOC_ROWS
    return pl.pallas_call(
        functools.partial(order_kernel, IN[n], items),
        out_shape=jax.ShapeDtypeStruct((total, HEAD_DIM), BF16),
        in_specs=[SMEM] + [VMEM] * GROUP,
        out_specs=VMEM,
        scratch_shapes=[pltpu.SemaphoreType.DMA((GROUP * len(items),))],
        compiler_params=SMALL,
        name=f"order_{chunk}",
    )(y, *arrived[n])


def dot(a, b, ca, cb):
    return lax.dot_general(a, b, (((ca,), (cb,)), ((), ())), preferred_element_type=F32)


def attend_kernel(offsets, sc_ref, starts_ref, own_ref, prev_ref, m0, m1, m2, m3, *refs):
    od_ref, back_ref, keep_ref, kw, vw, kt, vt, qs, gs, st, dp, dk, dv = refs[-13:]
    y = sc_ref[0]
    query_row = lax.broadcasted_iota(jnp.int32, (1, ROWS), 1)

    def runs(low, high, body, carry):
        at = low
        for size in RUNS:
            count = (high - at) // size
            carry = lax.fori_loop(
                0, count, lambda n, c, at=at, size=size: body(at + n * size, size, c), carry)
            at = at + count * size
        return carry

    def tiles(j, size):
        return pl.ds(pl.multiple_of(j * ROWS, ROWS), size * ROWS)

    for h in range(len(offsets)):
        base = 2 * h * SPAN
        for n in range(2 * GROUP):
            side = prev_ref if n < GROUP else own_ref
            at = base + n % GROUP * ROWS
            k_n = side[pl.ds(at, ROWS)]
            v_n = side[pl.ds(SPAN + at, ROWS)]
            kw[pl.ds(n * ROWS, ROWS)] = k_n
            vw[pl.ds(n * ROWS, ROWS)] = v_n
            kt[n] = k_n.T
            vt[n] = v_n.T
        for s, ref in enumerate((m0, m1, m2, m3)):
            at = pl.multiple_of(turned(y, -s) * ROWS, ROWS)
            qs[pl.ds(at, ROWS)] = ref[pl.ds(offsets[h][0], ROWS)]
            gs[pl.ds(at, ROWS)] = ref[pl.ds(offsets[h][1], ROWS)]
        dk[...] = jnp.zeros_like(dk)
        dv[...] = jnp.zeros_like(dv)

        for i in range(GROUP):
            block = pl.ds(i * ROWS, ROWS)
            q_i = qs[block]
            g_i = gs[block]
            start = starts_ref[:, block]
            last = query_row + (SPAN + i * ROWS)
            low = jnp.maximum(sc_ref[1 + i], i)
            high = GROUP + i + 1

            def score(j, size, top):
                first = j * ROWS
                key_row = lax.broadcasted_iota(jnp.int32, (size * ROWS, ROWS), 0)
                seen = (key_row >= start - first) & (key_row <= last - first)
                s = dot(kw[tiles(j, size)], q_i, 1, 1) * (SCALE * LOG2E)
                s = jnp.where(seen, s, -1e30)
                st[tiles(j - i, size)] = s
                dp[tiles(j - i, size)] = dot(vw[tiles(j, size)], g_i, 1, 1)
                return jnp.maximum(top, jnp.max(s, axis=0, keepdims=True))

            top = runs(low, high, score, jnp.full((1, ROWS), -1e30, F32))

            def forward(j, size, carry):
                total, acc = carry
                e = jnp.exp2(st[tiles(j - i, size)] - top)
                st[tiles(j - i, size)] = e
                low_e = e.astype(BF16)
                for m in range(size):
                    acc = acc + dot(vt[j + m], low_e[m * ROWS:(m + 1) * ROWS], 1, 0)
                return total + jnp.sum(e, axis=0, keepdims=True), acc

            total, acc = runs(
                low, high, forward,
                (jnp.zeros((1, ROWS), F32), jnp.zeros((HEAD_DIM, ROWS), F32)))
            inverse = 1.0 / total
            o_t = (acc * inverse).astype(BF16).astype(F32)
            delta = jnp.sum(o_t * g_i.astype(F32).T, axis=0, keepdims=True)
            od_ref[pl.ds(base + i * ROWS, ROWS)] = o_t.T.astype(BF16)

            def backward(j, size, acc):
                p = st[tiles(j - i, size)] * inverse
                ds = (p * (dp[tiles(j - i, size)] - delta)).astype(BF16)
                dv[tiles(j, size)] += dot(p.astype(BF16), g_i, 1, 0)
                dk[tiles(j, size)] += dot(ds, q_i, 1, 0)
                for m in range(size):
                    acc = acc + dot(kt[j + m], ds[m * ROWS:(m + 1) * ROWS], 1, 0)
                return acc

            dq_t = runs(low, high, backward, jnp.zeros((HEAD_DIM, ROWS), F32)) * SCALE
            od_ref[pl.ds(base + SPAN + i * ROWS, ROWS)] = dq_t.T.astype(BF16)

        for ref, at in ((back_ref, 0), (keep_ref, SPAN)):
            ref[pl.ds(base, SPAN)] = (dk[pl.ds(at, SPAN)] * SCALE).astype(BF16)
            ref[pl.ds(base + SPAN, SPAN)] = dv[pl.ds(at, SPAN)].astype(BF16)


def attend(chunk, scalars, starts, own, prev, arrived, earlier):
    heads = CHUNKS[chunk]
    n = holder(IN, ("q", heads[0]))
    offsets = [(offset(IN[n], ("q", h)), offset(IN[n], ("g", h))) for h in heads]
    window = pltpu.VMEM((2 * SPAN, HEAD_DIM), BF16)
    window_t = pltpu.VMEM((2 * GROUP, HEAD_DIM, ROWS), BF16)
    rows = pltpu.VMEM((SPAN, HEAD_DIM), BF16)
    scores = pltpu.VMEM(((GROUP + 1) * ROWS, ROWS), F32)
    total = pltpu.VMEM((2 * SPAN, HEAD_DIM), F32)
    return pl.pallas_call(
        functools.partial(attend_kernel, offsets),
        out_shape=[jax.ShapeDtypeStruct((2 * len(heads) * SPAN, HEAD_DIM), BF16)] * 3,
        in_specs=[SMEM] + [VMEM] * (3 + GROUP) + [ANY] * len(earlier),
        out_specs=[VMEM] * 3,
        scratch_shapes=[window, window, window_t, window_t, rows, rows, scores, scores, total, total],
        compiler_params=LARGE,
        name=f"attend_{chunk}",
    )(scalars, starts, own, prev, *arrived[n], *earlier)


def finish_kernel(plan, count, y_ref, *refs):
    y = y_ref[0]
    ins, outs = refs[:count], refs[-GROUP:]
    for s, out in enumerate(outs):
        for n, (sources, base) in enumerate(plan):
            rows = pl.ds(pl.multiple_of(base * SPAN + turned(y, s) * ROWS, ROWS), ROWS)
            value = ins[sources[0]][rows]
            if len(sources) == 2:
                value = (value.astype(F32) + ins[sources[1]][rows].astype(F32)).astype(BF16)
            out[pl.ds(n * ROWS, ROWS)] = value


def finish(n, y, done, returned, earlier):
    arrays, plan = [], []

    def index(key, array):
        for at, (other, _) in enumerate(arrays):
            if other == key:
                return at
        arrays.append((key, array))
        return len(arrays) - 1

    for name, h in OUT[n]:
        chunk = next(c for c, heads in enumerate(CHUNKS) if h in heads)
        base = 2 * CHUNKS[chunk].index(h) + (name in ("dq", "dv"))
        if name in ("o", "dq"):
            sources = (index((chunk, 0), done[chunk][0]),)
        else:
            sources = (index((chunk, 1), done[chunk][2]), index((chunk, 2), returned[chunk]))
        plan.append((sources, base))
    return pl.pallas_call(
        functools.partial(finish_kernel, plan, len(arrays)),
        out_shape=[jax.ShapeDtypeStruct((length(OUT[n]), HEAD_DIM), BF16)] * GROUP,
        in_specs=[SMEM] + [VMEM] * len(arrays) + [ANY] * len(earlier),
        out_specs=[VMEM] * GROUP,
        compiler_params=SMALL,
        name=f"finish_{n}",
    )(y, *[array for _, array in arrays], *earlier)


def unpack_kernel(messages, first, y_ref, *refs):
    pieces = refs[: GROUP * len(messages)]
    *outs, sem = refs[GROUP * len(messages) + (0 if first else len(RESULTS)):]
    y = y_ref[0]
    pairs = []
    for n, message in enumerate(messages):
        for s in range(GROUP):
            for item in message:
                name, h = item
                column = pl.multiple_of(turned(y, -s) * WIDTH + h * HEAD_DIM, HEAD_DIM)
                pairs.append((pieces[n * GROUP + s].at[pl.ds(offset(message, item), ROWS)],
                              outs[RESULTS.index(name)].at[:, pl.ds(column, HEAD_DIM)]))
    run_copies(pairs, sem)


def unpack(n, y, landed, outs):
    messages = [OUT[m] for m in UNPACK[n]]
    first = outs is None
    pieces = [piece for m in UNPACK[n] for piece in landed[m]]
    count = len(pieces)
    return pl.pallas_call(
        functools.partial(unpack_kernel, messages, first),
        out_shape=[jax.ShapeDtypeStruct((ROWS, HEADS * HEAD_DIM), BF16)] * len(RESULTS),
        in_specs=[SMEM] + [VMEM] * count + ([] if first else [HBM] * len(RESULTS)),
        out_specs=[HBM] * len(RESULTS),
        scratch_shapes=[pltpu.SemaphoreType.DMA((GROUP * sum(map(len, messages)),))],
        input_output_aliases={} if first else {1 + count + r: r for r in range(len(RESULTS))},
        compiler_params=SMALL,
        name=f"unpack_{n}",
    )(y, *pieces, *(() if first else outs))


def exchange(pieces):
    return [pieces[0]] + [shift_y(pieces[s], s) for s in range(1, GROUP)]


def document_rows(message):
    tail = message[message.shape[0] - GROUP * DOC_ROWS:]
    tail = tail.reshape(GROUP, DOC_ROWS, HEAD_DIM)[:, : ROWS // HEAD_DIM]
    return tail.reshape(SPAN).astype(jnp.int32)


def shards(queries, keys, values, out_grad, doc_ids):
    device = lax.axis_index(AXES)
    y = lax.rem(device, GROUP).astype(jnp.int32).reshape(1)
    docs = jnp.tile(doc_ids.astype(BF16).reshape(ROWS // HEAD_DIM, HEAD_DIM),
                    (DOC_ROWS * HEAD_DIM // ROWS, 1))
    chunks = range(len(CHUNKS))
    arrays = (keys, values, queries, out_grad, docs)
    packed = pack(IN[:1], y, *arrays) + pack(IN[1:], y, *arrays)
    arrived = [exchange(p) for p in packed]
    ordered = [order(c, y, arrived) for c in chunks]
    behind = {0: [shift_group(piece, 1) for piece in arrived[0]]}
    previous = [order(c, y, behind) if c == 0 else shift_group(ordered[c], 1) for c in chunks]

    own_docs = document_rows(ordered[0])
    prev_docs = jnp.where(device >= GROUP, document_rows(previous[0]), -1)
    window = jnp.concatenate([prev_docs, own_docs])
    starts = jnp.sum((window[None, :] < own_docs[:, None]).astype(jnp.int32), axis=1)
    scalars = jnp.concatenate([y, starts[::ROWS] // ROWS])
    starts = starts.reshape(1, SPAN)

    done = [attend(c, scalars, starts, ordered[c], previous[c], arrived, ordered[c + 1: c + 2])
            for c in chunks]
    returned = [shift_group(d[1], -1) for d in done]
    landed = []
    for n in range(len(OUT)):
        earlier = landed[AFTER[n]][1:] if AFTER[n] is not None else []
        landed.append(exchange(finish(n, y, done, returned, earlier)))
    outs = None
    for n in range(len(UNPACK)):
        outs = unpack(n, y, landed, outs)
    return tuple(outs)


def solution(mesh):
    rows = P(AXES, None)
    return jax.shard_map(
        shards,
        mesh=mesh,
        in_specs=(rows, rows, rows, rows, P(AXES)),
        out_specs=(rows, rows, rows, rows),
        check_vma=False,
    )
```

```python
import functools
import math

import jax
import jax.numpy as jnp
from jax import lax
from jax.experimental import pallas as pl
from jax.experimental.pallas import tpu as pltpu
from jax.sharding import PartitionSpec as P

HEADS = 16
HEAD_DIM = 128
ROWS = 256
GROUP = 4
SPAN = GROUP * ROWS
DOC_ROWS = 16
SCALE = 1.0 / math.sqrt(HEAD_DIM)
LOG2E = math.log2(math.e)
AXES = ("grp", "seq")
BF16 = jnp.bfloat16
F32 = jnp.float32
SMEM = pl.BlockSpec(memory_space=pltpu.SMEM)
VMEM = pl.BlockSpec(memory_space=pltpu.VMEM)
ANY = pl.BlockSpec(memory_space=pl.ANY)
HBM = pl.BlockSpec(memory_space=pltpu.HBM)
SMALL = pltpu.CompilerParams(vmem_limit_bytes=8 * 1024 * 1024)
WHOLE = pltpu.CompilerParams(vmem_limit_bytes=56 * 1024 * 1024)
LARGE = pltpu.CompilerParams(vmem_limit_bytes=12 * 1024 * 1024)
CHUNKS = ((0,), (1,), (2,), (3,))
IN = (
    (("k", 0), ("v", 0), ("doc", 0),),
    (("q", 0), ("g", 0), ("k", 1), ("v", 1),),
    (("q", 1), ("g", 1), ("k", 2), ("v", 2), ("q", 2), ("g", 2), ("k", 3), ("v", 3), ("q", 3), ("g", 3),),
)
OUT = (
    (("o", 0), ("dq", 0), ("o", 1), ("dq", 1), ("dk", 0), ("dv", 0),),
    (("dk", 1), ("dv", 1), ("o", 2), ("dq", 2), ("o", 3), ("dq", 3),),
    (("dk", 2), ("dv", 2), ("dk", 3), ("dv", 3),),
)
UNPACK = ((0, 1), (2,))
AFTER = (None, 0, None)
LATER = ((1,), (2,), (3,), ())
RUNS = (3, 2, 1)
RESULTS = ("o", "dq", "dk", "dv")
WIDTH = HEADS // GROUP * HEAD_DIM


def shift_y(block, step):
    total = lax.axis_size(AXES)
    route = [(d, d // GROUP * GROUP + (d + step) % GROUP) for d in range(total)]
    return lax.ppermute(block, AXES, route)


def shift_group(block, step):
    total = lax.axis_size(AXES)
    route = [(d, (d + step * GROUP) % total) for d in range(total)]
    return lax.ppermute(block, AXES, route)


def run_copies(pairs, sem):
    copies = [pltpu.make_async_copy(src, dst, sem.at[n]) for n, (src, dst) in enumerate(pairs)]
    for copy in copies:
        copy.start()
    for copy in copies:
        copy.wait()


def rows_of(item):
    return DOC_ROWS if item[0] == "doc" else ROWS


def length(message):
    return sum(rows_of(item) for item in message)


def offset(message, item):
    return length(message[: message.index(item)])


def holder(messages, item):
    return next(n for n, message in enumerate(messages) if item in message)


def turned(y, s):
    return lax.rem(y + s + GROUP, GROUP)


def pack_kernel(messages, y_ref, k_ref, v_ref, q_ref, g_ref, doc_ref, *refs):
    *outs, sem = refs
    y = y_ref[0]
    source = {"k": k_ref, "v": v_ref, "q": q_ref, "g": g_ref}
    pairs = []
    for n, message in enumerate(messages):
        for s in range(GROUP):
            for item in message:
                name, h = item
                rows = outs[n * GROUP + s].at[pl.ds(offset(message, item), rows_of(item))]
                if name == "doc":
                    pairs.append((doc_ref, rows))
                    continue
                column = pl.multiple_of(turned(y, s) * WIDTH + h * HEAD_DIM, HEAD_DIM)
                pairs.append((source[name].at[:, pl.ds(column, HEAD_DIM)], rows))
    run_copies(pairs, sem)


def pack(messages, y, k, v, q, g, docs):
    pieces = pl.pallas_call(
        functools.partial(pack_kernel, messages),
        out_shape=[jax.ShapeDtypeStruct((length(message), HEAD_DIM), BF16)
                   for message in messages for _ in range(GROUP)],
        in_specs=[SMEM] + [HBM] * 5,
        out_specs=[VMEM] * (GROUP * len(messages)),
        scratch_shapes=[pltpu.SemaphoreType.DMA((GROUP * sum(map(len, messages)),))],
        compiler_params=WHOLE,
        name="pack",
    )(y, k, v, q, g, docs)
    return [pieces[n * GROUP: (n + 1) * GROUP] for n in range(len(messages))]


def order_kernel(message, items, y_ref, m0, m1, m2, m3, out, sem):
    y = y_ref[0]
    pairs = []
    for s, ref in enumerate((m0, m1, m2, m3)):
        at = turned(y, -s)
        for n, item in enumerate(items):
            size = rows_of(item)
            place = pl.multiple_of(n * SPAN + at * size, size)
            pairs.append((ref.at[pl.ds(offset(message, item), size)], out.at[pl.ds(place, size)]))
    run_copies(pairs, sem)


def order(chunk, y, arrived):
    items = [(name, h) for h in CHUNKS[chunk] for name in ("k", "v")]
    n = holder(IN, items[0])
    total = len(items) * SPAN
    if chunk == 0:
        items.append(("doc", 0))
        total += GROUP * DOC_ROWS
    return pl.pallas_call(
        functools.partial(order_kernel, IN[n], items),
        out_shape=jax.ShapeDtypeStruct((total, HEAD_DIM), BF16),
        in_specs=[SMEM] + [VMEM] * GROUP,
        out_specs=VMEM,
        scratch_shapes=[pltpu.SemaphoreType.DMA((GROUP * len(items),))],
        compiler_params=SMALL,
        name=f"order_{chunk}",
    )(y, *arrived[n])


def dot(a, b, ca, cb):
    return lax.dot_general(a, b, (((ca,), (cb,)), ((), ())), preferred_element_type=F32)


def attend_kernel(offsets, sc_ref, starts_ref, own_ref, prev_ref, m0, m1, m2, m3, *refs):
    od_ref, back_ref, keep_ref, kw, vw, kt, vt, qs, gs, st, dp, dk, dv = refs[-13:]
    y = sc_ref[0]
    query_row = lax.broadcasted_iota(jnp.int32, (1, ROWS), 1)

    def runs(low, high, body, carry):
        at = low
        for size in RUNS:
            count = (high - at) // size
            carry = lax.fori_loop(
                0, count, lambda n, c, at=at, size=size: body(at + n * size, size, c), carry)
            at = at + count * size
        return carry

    def tiles(j, size):
        return pl.ds(pl.multiple_of(j * ROWS, ROWS), size * ROWS)

    for h in range(len(offsets)):
        base = 2 * h * SPAN
        for n in range(2 * GROUP):
            side = prev_ref if n < GROUP else own_ref
            at = base + n % GROUP * ROWS
            k_n = side[pl.ds(at, ROWS)]
            v_n = side[pl.ds(SPAN + at, ROWS)]
            kw[pl.ds(n * ROWS, ROWS)] = k_n
            vw[pl.ds(n * ROWS, ROWS)] = v_n
            kt[n] = k_n.T
            vt[n] = v_n.T
        for s, ref in enumerate((m0, m1, m2, m3)):
            at = pl.multiple_of(turned(y, -s) * ROWS, ROWS)
            qs[pl.ds(at, ROWS)] = ref[pl.ds(offsets[h][0], ROWS)]
            gs[pl.ds(at, ROWS)] = ref[pl.ds(offsets[h][1], ROWS)]
        dk[...] = jnp.zeros_like(dk)
        dv[...] = jnp.zeros_like(dv)

        for i in range(GROUP):
            block = pl.ds(i * ROWS, ROWS)
            q_i = qs[block]
            g_i = gs[block]
            start = starts_ref[:, block]
            last = query_row + (SPAN + i * ROWS)
            low = jnp.maximum(sc_ref[1 + i], i)
            high = GROUP + i + 1

            def score(j, size, top):
                first = j * ROWS
                key_row = lax.broadcasted_iota(jnp.int32, (size * ROWS, ROWS), 0)
                seen = (key_row >= start - first) & (key_row <= last - first)
                s = dot(kw[tiles(j, size)], q_i, 1, 1) * (SCALE * LOG2E)
                s = jnp.where(seen, s, -1e30)
                st[tiles(j - i, size)] = s
                dp[tiles(j - i, size)] = dot(vw[tiles(j, size)], g_i, 1, 1)
                return jnp.maximum(top, jnp.max(s, axis=0, keepdims=True))

            top = runs(low, high, score, jnp.full((1, ROWS), -1e30, F32))

            def forward(j, size, carry):
                total, acc = carry
                e = jnp.exp2(st[tiles(j - i, size)] - top)
                st[tiles(j - i, size)] = e
                low_e = e.astype(BF16)
                for m in range(size):
                    acc = acc + dot(vt[j + m], low_e[m * ROWS:(m + 1) * ROWS], 1, 0)
                return total + jnp.sum(e, axis=0, keepdims=True), acc

            total, acc = runs(
                low, high, forward,
                (jnp.zeros((1, ROWS), F32), jnp.zeros((HEAD_DIM, ROWS), F32)))
            inverse = 1.0 / total
            o_t = (acc * inverse).astype(BF16).astype(F32)
            delta = jnp.sum(o_t * g_i.astype(F32).T, axis=0, keepdims=True)
            od_ref[pl.ds(base + i * ROWS, ROWS)] = o_t.T.astype(BF16)

            def backward(j, size, acc):
                p = st[tiles(j - i, size)] * inverse
                ds = (p * (dp[tiles(j - i, size)] - delta)).astype(BF16)
                dv[tiles(j, size)] += dot(p.astype(BF16), g_i, 1, 0)
                dk[tiles(j, size)] += dot(ds, q_i, 1, 0)
                for m in range(size):
                    acc = acc + dot(kt[j + m], ds[m * ROWS:(m + 1) * ROWS], 1, 0)
                return acc

            dq_t = runs(low, high, backward, jnp.zeros((HEAD_DIM, ROWS), F32)) * SCALE
            od_ref[pl.ds(base + SPAN + i * ROWS, ROWS)] = dq_t.T.astype(BF16)

        for ref, at in ((back_ref, 0), (keep_ref, SPAN)):
            ref[pl.ds(base, SPAN)] = (dk[pl.ds(at, SPAN)] * SCALE).astype(BF16)
            ref[pl.ds(base + SPAN, SPAN)] = dv[pl.ds(at, SPAN)].astype(BF16)


def attend(chunk, scalars, starts, own, prev, arrived, earlier):
    heads = CHUNKS[chunk]
    n = holder(IN, ("q", heads[0]))
    offsets = [(offset(IN[n], ("q", h)), offset(IN[n], ("g", h))) for h in heads]
    window = pltpu.VMEM((2 * SPAN, HEAD_DIM), BF16)
    window_t = pltpu.VMEM((2 * GROUP, HEAD_DIM, ROWS), BF16)
    rows = pltpu.VMEM((SPAN, HEAD_DIM), BF16)
    scores = pltpu.VMEM(((GROUP + 1) * ROWS, ROWS), F32)
    total = pltpu.VMEM((2 * SPAN, HEAD_DIM), F32)
    return pl.pallas_call(
        functools.partial(attend_kernel, offsets),
        out_shape=[jax.ShapeDtypeStruct((2 * len(heads) * SPAN, HEAD_DIM), BF16)] * 3,
        in_specs=[SMEM] + [VMEM] * (3 + GROUP) + [ANY] * len(earlier),
        out_specs=[VMEM] * 3,
        scratch_shapes=[window, window, window_t, window_t, rows, rows, scores, scores, total, total],
        compiler_params=LARGE,
        name=f"attend_{chunk}",
    )(scalars, starts, own, prev, *arrived[n], *earlier)


def finish_kernel(plan, count, y_ref, *refs):
    y = y_ref[0]
    ins, outs = refs[:count], refs[-GROUP:]
    for s, out in enumerate(outs):
        for n, (sources, base) in enumerate(plan):
            rows = pl.ds(pl.multiple_of(base * SPAN + turned(y, s) * ROWS, ROWS), ROWS)
            value = ins[sources[0]][rows]
            if len(sources) == 2:
                value = (value.astype(F32) + ins[sources[1]][rows].astype(F32)).astype(BF16)
            out[pl.ds(n * ROWS, ROWS)] = value


def finish(n, y, done, returned, earlier):
    arrays, plan = [], []

    def index(key, array):
        for at, (other, _) in enumerate(arrays):
            if other == key:
                return at
        arrays.append((key, array))
        return len(arrays) - 1

    for name, h in OUT[n]:
        chunk = next(c for c, heads in enumerate(CHUNKS) if h in heads)
        base = 2 * CHUNKS[chunk].index(h) + (name in ("dq", "dv"))
        if name in ("o", "dq"):
            sources = (index((chunk, 0), done[chunk][0]),)
        else:
            sources = (index((chunk, 1), done[chunk][2]), index((chunk, 2), returned[chunk]))
        plan.append((sources, base))
    return pl.pallas_call(
        functools.partial(finish_kernel, plan, len(arrays)),
        out_shape=[jax.ShapeDtypeStruct((length(OUT[n]), HEAD_DIM), BF16)] * GROUP,
        in_specs=[SMEM] + [VMEM] * len(arrays) + [ANY] * len(earlier),
        out_specs=[VMEM] * GROUP,
        compiler_params=SMALL,
        name=f"finish_{n}",
    )(y, *[array for _, array in arrays], *earlier)


def unpack_kernel(messages, first, y_ref, *refs):
    pieces = refs[: GROUP * len(messages)]
    *outs, sem = refs[GROUP * len(messages) + (0 if first else len(RESULTS)):]
    y = y_ref[0]
    pairs = []
    for n, message in enumerate(messages):
        for s in range(GROUP):
            for item in message:
                name, h = item
                column = pl.multiple_of(turned(y, -s) * WIDTH + h * HEAD_DIM, HEAD_DIM)
                pairs.append((pieces[n * GROUP + s].at[pl.ds(offset(message, item), ROWS)],
                              outs[RESULTS.index(name)].at[:, pl.ds(column, HEAD_DIM)]))
    run_copies(pairs, sem)


def unpack(n, y, landed, outs):
    messages = [OUT[m] for m in UNPACK[n]]
    first = outs is None
    pieces = [piece for m in UNPACK[n] for piece in landed[m]]
    count = len(pieces)
    return pl.pallas_call(
        functools.partial(unpack_kernel, messages, first),
        out_shape=[jax.ShapeDtypeStruct((ROWS, HEADS * HEAD_DIM), BF16)] * len(RESULTS),
        in_specs=[SMEM] + [VMEM] * count + ([] if first else [HBM] * len(RESULTS)),
        out_specs=[HBM] * len(RESULTS),
        scratch_shapes=[pltpu.SemaphoreType.DMA((GROUP * sum(map(len, messages)),))],
        input_output_aliases={} if first else {1 + count + r: r for r in range(len(RESULTS))},
        compiler_params=SMALL,
        name=f"unpack_{n}",
    )(y, *pieces, *(() if first else outs))


def exchange(pieces):
    return [pieces[0]] + [shift_y(pieces[s], s) for s in range(1, GROUP)]


def document_rows(message):
    tail = message[message.shape[0] - GROUP * DOC_ROWS:]
    tail = tail.reshape(GROUP, DOC_ROWS, HEAD_DIM)[:, : ROWS // HEAD_DIM]
    return tail.reshape(SPAN).astype(jnp.int32)


def shards(queries, keys, values, out_grad, doc_ids):
    device = lax.axis_index(AXES)
    y = lax.rem(device, GROUP).astype(jnp.int32).reshape(1)
    docs = jnp.tile(doc_ids.astype(BF16).reshape(ROWS // HEAD_DIM, HEAD_DIM),
                    (DOC_ROWS * HEAD_DIM // ROWS, 1))
    chunks = range(len(CHUNKS))
    arrays = (keys, values, queries, out_grad, docs)
    packed = pack(IN, y, *arrays)
    arrived = [exchange(p) for p in packed]
    ordered = [order(c, y, arrived) for c in chunks]
    behind = {0: [shift_group(piece, 1) for piece in arrived[0]]}
    previous = [order(c, y, behind) if c == 0 else shift_group(ordered[c], 1) for c in chunks]

    own_docs = document_rows(ordered[0])
    within = jnp.sum((own_docs[None, :] < own_docs[:, None]).astype(jnp.int32), axis=1)
    prev_docs = jnp.where(device >= GROUP, document_rows(previous[0]), -1)
    before = jnp.sum((prev_docs < own_docs[0]).astype(jnp.int32))
    starts = within + jnp.where(own_docs == own_docs[0], before, SPAN)
    scalars = jnp.concatenate([y, starts.reshape(GROUP, ROWS)[:, 0] // ROWS])
    starts = starts.reshape(1, SPAN)

    done = [attend(c, scalars, starts, ordered[c], previous[c], arrived, [ordered[n] for n in LATER[c]])
            for c in chunks]
    returned = [shift_group(d[1], -1) for d in done]
    landed = []
    for n in range(len(OUT)):
        earlier = landed[AFTER[n]][1:] if AFTER[n] is not None else []
        landed.append(exchange(finish(n, y, done, returned, earlier)))
    outs = None
    for n in range(len(UNPACK)):
        outs = unpack(n, y, landed, outs)
    return tuple(outs)


def solution(mesh):
    rows = P(AXES, None)
    return jax.shard_map(
        shards,
        mesh=mesh,
        in_specs=(rows, rows, rows, rows, P(AXES)),
        out_specs=(rows, rows, rows, rows),
        check_vma=False,
    )
```

```python
import functools
import math

import jax
import jax.numpy as jnp
from jax import lax
from jax.experimental import pallas as pl
from jax.experimental.pallas import tpu as pltpu
from jax.sharding import PartitionSpec as P

HEADS = 16
HEAD_DIM = 128
ROWS = 256
GROUP = 4
SPAN = GROUP * ROWS
DOC_ROWS = 16
SCALE = 1.0 / math.sqrt(HEAD_DIM)
LOG2E = math.log2(math.e)
AXES = ("grp", "seq")
BF16 = jnp.bfloat16
F32 = jnp.float32
SMEM = pl.BlockSpec(memory_space=pltpu.SMEM)
VMEM = pl.BlockSpec(memory_space=pltpu.VMEM)
ANY = pl.BlockSpec(memory_space=pl.ANY)
HBM = pl.BlockSpec(memory_space=pltpu.HBM)
SMALL = pltpu.CompilerParams(vmem_limit_bytes=8 * 1024 * 1024)
WHOLE = pltpu.CompilerParams(vmem_limit_bytes=56 * 1024 * 1024)
LARGE = pltpu.CompilerParams(vmem_limit_bytes=12 * 1024 * 1024)
CHUNKS = ((0,), (1,), (2,), (3,))
IN = (
    (("k", 0), ("v", 0), ("doc", 0),),
    (("q", 0), ("g", 0), ("k", 1), ("v", 1),),
    (("q", 1), ("g", 1), ("k", 2), ("v", 2), ("k", 3), ("v", 3),),
    (("q", 2), ("g", 2), ("q", 3), ("g", 3),),
)
OUT = (
    (("o", 0), ("dq", 0), ("o", 1), ("dq", 1), ("dk", 0), ("dv", 0),),
    (("dk", 1), ("dv", 1), ("o", 2), ("dq", 2), ("o", 3), ("dq", 3),),
    (("dk", 2), ("dv", 2), ("dk", 3), ("dv", 3),),
)
UNPACK = ((0, 1), (2,))
AFTER = (None, 0, None)
LATER = ((1,), (2,), (3,), ())
RUNS = (3, 2, 1)
RESULTS = ("o", "dq", "dk", "dv")
WIDTH = HEADS // GROUP * HEAD_DIM


def shift_y(block, step):
    total = lax.axis_size(AXES)
    route = [(d, d // GROUP * GROUP + (d + step) % GROUP) for d in range(total)]
    return lax.ppermute(block, AXES, route)


def shift_group(block, step):
    total = lax.axis_size(AXES)
    route = [(d, (d + step * GROUP) % total) for d in range(total)]
    return lax.ppermute(block, AXES, route)


def run_copies(pairs, sem):
    copies = [pltpu.make_async_copy(src, dst, sem.at[n]) for n, (src, dst) in enumerate(pairs)]
    for copy in copies:
        copy.start()
    for copy in copies:
        copy.wait()


def rows_of(item):
    return DOC_ROWS if item[0] == "doc" else ROWS


def length(message):
    return sum(rows_of(item) for item in message)


def offset(message, item):
    return length(message[: message.index(item)])


def holder(messages, item):
    return next(n for n, message in enumerate(messages) if item in message)


def turned(y, s):
    return lax.rem(y + s + GROUP, GROUP)


def pack_kernel(messages, y_ref, k_ref, v_ref, q_ref, g_ref, doc_ref, *refs):
    *outs, sem = refs
    y = y_ref[0]
    source = {"k": k_ref, "v": v_ref, "q": q_ref, "g": g_ref}
    pairs = []
    for n, message in enumerate(messages):
        for s in range(GROUP):
            for item in message:
                name, h = item
                rows = outs[n * GROUP + s].at[pl.ds(offset(message, item), rows_of(item))]
                if name == "doc":
                    pairs.append((doc_ref, rows))
                    continue
                column = pl.multiple_of(turned(y, s) * WIDTH + h * HEAD_DIM, HEAD_DIM)
                pairs.append((source[name].at[:, pl.ds(column, HEAD_DIM)], rows))
    run_copies(pairs, sem)


def pack(messages, y, k, v, q, g, docs):
    pieces = pl.pallas_call(
        functools.partial(pack_kernel, messages),
        out_shape=[jax.ShapeDtypeStruct((length(message), HEAD_DIM), BF16)
                   for message in messages for _ in range(GROUP)],
        in_specs=[SMEM] + [HBM] * 5,
        out_specs=[VMEM] * (GROUP * len(messages)),
        scratch_shapes=[pltpu.SemaphoreType.DMA((GROUP * sum(map(len, messages)),))],
        compiler_params=WHOLE,
        name="pack",
    )(y, k, v, q, g, docs)
    return [pieces[n * GROUP: (n + 1) * GROUP] for n in range(len(messages))]


def order_kernel(message, items, y_ref, m0, m1, m2, m3, out, sem):
    y = y_ref[0]
    pairs = []
    for s, ref in enumerate((m0, m1, m2, m3)):
        at = turned(y, -s)
        for n, item in enumerate(items):
            size = rows_of(item)
            place = pl.multiple_of(n * SPAN + at * size, size)
            pairs.append((ref.at[pl.ds(offset(message, item), size)], out.at[pl.ds(place, size)]))
    run_copies(pairs, sem)


def order(chunk, y, arrived):
    items = [(name, h) for h in CHUNKS[chunk] for name in ("k", "v")]
    n = holder(IN, items[0])
    total = len(items) * SPAN
    if chunk == 0:
        items.append(("doc", 0))
        total += GROUP * DOC_ROWS
    return pl.pallas_call(
        functools.partial(order_kernel, IN[n], items),
        out_shape=jax.ShapeDtypeStruct((total, HEAD_DIM), BF16),
        in_specs=[SMEM] + [VMEM] * GROUP,
        out_specs=VMEM,
        scratch_shapes=[pltpu.SemaphoreType.DMA((GROUP * len(items),))],
        compiler_params=SMALL,
        name=f"order_{chunk}",
    )(y, *arrived[n])


def dot(a, b, ca, cb):
    return lax.dot_general(a, b, (((ca,), (cb,)), ((), ())), preferred_element_type=F32)


def attend_kernel(offsets, sc_ref, starts_ref, own_ref, prev_ref, m0, m1, m2, m3, *refs):
    od_ref, back_ref, keep_ref, kw, vw, kt, vt, qs, gs, st, dp, dk, dv = refs[-13:]
    y = sc_ref[0]
    query_row = lax.broadcasted_iota(jnp.int32, (1, ROWS), 1)

    def runs(low, high, body, carry):
        at = low
        for size in RUNS:
            count = (high - at) // size
            carry = lax.fori_loop(
                0, count, lambda n, c, at=at, size=size: body(at + n * size, size, c), carry)
            at = at + count * size
        return carry

    def tiles(j, size):
        return pl.ds(pl.multiple_of(j * ROWS, ROWS), size * ROWS)

    for h in range(len(offsets)):
        base = 2 * h * SPAN
        for n in range(2 * GROUP):
            side = prev_ref if n < GROUP else own_ref
            at = base + n % GROUP * ROWS
            k_n = side[pl.ds(at, ROWS)]
            v_n = side[pl.ds(SPAN + at, ROWS)]
            kw[pl.ds(n * ROWS, ROWS)] = k_n
            vw[pl.ds(n * ROWS, ROWS)] = v_n
            kt[n] = k_n.T
            vt[n] = v_n.T
        for s, ref in enumerate((m0, m1, m2, m3)):
            at = pl.multiple_of(turned(y, -s) * ROWS, ROWS)
            qs[pl.ds(at, ROWS)] = ref[pl.ds(offsets[h][0], ROWS)]
            gs[pl.ds(at, ROWS)] = ref[pl.ds(offsets[h][1], ROWS)]
        dk[...] = jnp.zeros_like(dk)
        dv[...] = jnp.zeros_like(dv)

        for i in range(GROUP):
            block = pl.ds(i * ROWS, ROWS)
            q_i = qs[block]
            g_i = gs[block]
            start = starts_ref[:, block]
            last = query_row + (SPAN + i * ROWS)
            low = jnp.maximum(sc_ref[1 + i], i)
            high = GROUP + i + 1

            def score(j, size, top):
                first = j * ROWS
                key_row = lax.broadcasted_iota(jnp.int32, (size * ROWS, ROWS), 0)
                seen = (key_row >= start - first) & (key_row <= last - first)
                s = dot(kw[tiles(j, size)], q_i, 1, 1) * (SCALE * LOG2E)
                s = jnp.where(seen, s, -1e30)
                st[tiles(j - i, size)] = s
                dp[tiles(j - i, size)] = dot(vw[tiles(j, size)], g_i, 1, 1)
                return jnp.maximum(top, jnp.max(s, axis=0, keepdims=True))

            top = runs(low, high, score, jnp.full((1, ROWS), -1e30, F32))

            def forward(j, size, carry):
                total, acc = carry
                e = jnp.exp2(st[tiles(j - i, size)] - top)
                st[tiles(j - i, size)] = e
                low_e = e.astype(BF16)
                for m in range(size):
                    acc = acc + dot(vt[j + m], low_e[m * ROWS:(m + 1) * ROWS], 1, 0)
                return total + jnp.sum(e, axis=0, keepdims=True), acc

            total, acc = runs(
                low, high, forward,
                (jnp.zeros((1, ROWS), F32), jnp.zeros((HEAD_DIM, ROWS), F32)))
            inverse = 1.0 / total
            o_t = (acc * inverse).astype(BF16).astype(F32)
            delta = jnp.sum(o_t * g_i.astype(F32).T, axis=0, keepdims=True)
            od_ref[pl.ds(base + i * ROWS, ROWS)] = o_t.T.astype(BF16)

            def backward(j, size, acc):
                p = st[tiles(j - i, size)] * inverse
                ds = (p * (dp[tiles(j - i, size)] - delta)).astype(BF16)
                dv[tiles(j, size)] += dot(p.astype(BF16), g_i, 1, 0)
                dk[tiles(j, size)] += dot(ds, q_i, 1, 0)
                for m in range(size):
                    acc = acc + dot(kt[j + m], ds[m * ROWS:(m + 1) * ROWS], 1, 0)
                return acc

            dq_t = runs(low, high, backward, jnp.zeros((HEAD_DIM, ROWS), F32)) * SCALE
            od_ref[pl.ds(base + SPAN + i * ROWS, ROWS)] = dq_t.T.astype(BF16)

        for ref, at in ((back_ref, 0), (keep_ref, SPAN)):
            ref[pl.ds(base, SPAN)] = (dk[pl.ds(at, SPAN)] * SCALE).astype(BF16)
            ref[pl.ds(base + SPAN, SPAN)] = dv[pl.ds(at, SPAN)].astype(BF16)


def attend(chunk, scalars, starts, own, prev, arrived, earlier):
    heads = CHUNKS[chunk]
    n = holder(IN, ("q", heads[0]))
    offsets = [(offset(IN[n], ("q", h)), offset(IN[n], ("g", h))) for h in heads]
    window = pltpu.VMEM((2 * SPAN, HEAD_DIM), BF16)
    window_t = pltpu.VMEM((2 * GROUP, HEAD_DIM, ROWS), BF16)
    rows = pltpu.VMEM((SPAN, HEAD_DIM), BF16)
    scores = pltpu.VMEM(((GROUP + 1) * ROWS, ROWS), F32)
    total = pltpu.VMEM((2 * SPAN, HEAD_DIM), F32)
    return pl.pallas_call(
        functools.partial(attend_kernel, offsets),
        out_shape=[jax.ShapeDtypeStruct((2 * len(heads) * SPAN, HEAD_DIM), BF16)] * 3,
        in_specs=[SMEM] + [VMEM] * (3 + GROUP) + [ANY] * len(earlier),
        out_specs=[VMEM] * 3,
        scratch_shapes=[window, window, window_t, window_t, rows, rows, scores, scores, total, total],
        compiler_params=LARGE,
        name=f"attend_{chunk}",
    )(scalars, starts, own, prev, *arrived[n], *earlier)


def finish_kernel(plan, count, y_ref, *refs):
    y = y_ref[0]
    ins, outs = refs[:count], refs[-GROUP:]
    for s, out in enumerate(outs):
        for n, (sources, base) in enumerate(plan):
            rows = pl.ds(pl.multiple_of(base * SPAN + turned(y, s) * ROWS, ROWS), ROWS)
            value = ins[sources[0]][rows]
            if len(sources) == 2:
                value = (value.astype(F32) + ins[sources[1]][rows].astype(F32)).astype(BF16)
            out[pl.ds(n * ROWS, ROWS)] = value


def finish(n, y, done, returned, earlier):
    arrays, plan = [], []

    def index(key, array):
        for at, (other, _) in enumerate(arrays):
            if other == key:
                return at
        arrays.append((key, array))
        return len(arrays) - 1

    for name, h in OUT[n]:
        chunk = next(c for c, heads in enumerate(CHUNKS) if h in heads)
        base = 2 * CHUNKS[chunk].index(h) + (name in ("dq", "dv"))
        if name in ("o", "dq"):
            sources = (index((chunk, 0), done[chunk][0]),)
        else:
            sources = (index((chunk, 1), done[chunk][2]), index((chunk, 2), returned[chunk]))
        plan.append((sources, base))
    return pl.pallas_call(
        functools.partial(finish_kernel, plan, len(arrays)),
        out_shape=[jax.ShapeDtypeStruct((length(OUT[n]), HEAD_DIM), BF16)] * GROUP,
        in_specs=[SMEM] + [VMEM] * len(arrays) + [ANY] * len(earlier),
        out_specs=[VMEM] * GROUP,
        compiler_params=SMALL,
        name=f"finish_{n}",
    )(y, *[array for _, array in arrays], *earlier)


def unpack_kernel(messages, first, y_ref, *refs):
    pieces = refs[: GROUP * len(messages)]
    *outs, sem = refs[GROUP * len(messages) + (0 if first else len(RESULTS)):]
    y = y_ref[0]
    pairs = []
    for n, message in enumerate(messages):
        for s in range(GROUP):
            for item in message:
                name, h = item
                column = pl.multiple_of(turned(y, -s) * WIDTH + h * HEAD_DIM, HEAD_DIM)
                pairs.append((pieces[n * GROUP + s].at[pl.ds(offset(message, item), ROWS)],
                              outs[RESULTS.index(name)].at[:, pl.ds(column, HEAD_DIM)]))
    run_copies(pairs, sem)


def unpack(n, y, landed, outs):
    messages = [OUT[m] for m in UNPACK[n]]
    first = outs is None
    pieces = [piece for m in UNPACK[n] for piece in landed[m]]
    count = len(pieces)
    return pl.pallas_call(
        functools.partial(unpack_kernel, messages, first),
        out_shape=[jax.ShapeDtypeStruct((ROWS, HEADS * HEAD_DIM), BF16)] * len(RESULTS),
        in_specs=[SMEM] + [VMEM] * count + ([] if first else [HBM] * len(RESULTS)),
        out_specs=[HBM] * len(RESULTS),
        scratch_shapes=[pltpu.SemaphoreType.DMA((GROUP * sum(map(len, messages)),))],
        input_output_aliases={} if first else {1 + count + r: r for r in range(len(RESULTS))},
        compiler_params=SMALL,
        name=f"unpack_{n}",
    )(y, *pieces, *(() if first else outs))


def exchange(pieces):
    return [pieces[0]] + [shift_y(pieces[s], s) for s in range(1, GROUP)]


def document_rows(message):
    tail = message[message.shape[0] - GROUP * DOC_ROWS:]
    tail = tail.reshape(GROUP, DOC_ROWS, HEAD_DIM)[:, : ROWS // HEAD_DIM]
    return tail.reshape(SPAN).astype(jnp.int32)


def shards(queries, keys, values, out_grad, doc_ids):
    device = lax.axis_index(AXES)
    y = lax.rem(device, GROUP).astype(jnp.int32).reshape(1)
    docs = jnp.tile(doc_ids.astype(BF16).reshape(ROWS // HEAD_DIM, HEAD_DIM),
                    (DOC_ROWS * HEAD_DIM // ROWS, 1))
    chunks = range(len(CHUNKS))
    arrays = (keys, values, queries, out_grad, docs)
    packed = pack(IN, y, *arrays)
    arrived = [exchange(p) for p in packed]
    ordered = [order(c, y, arrived) for c in chunks]
    behind = {0: [shift_group(piece, 1) for piece in arrived[0]]}
    previous = [order(c, y, behind) if c == 0 else shift_group(ordered[c], 1) for c in chunks]

    own_docs = document_rows(ordered[0])
    within = jnp.sum((own_docs[None, :] < own_docs[:, None]).astype(jnp.int32), axis=1)
    prev_docs = jnp.where(device >= GROUP, document_rows(previous[0]), -1)
    before = jnp.sum((prev_docs < own_docs[0]).astype(jnp.int32))
    starts = within + jnp.where(own_docs == own_docs[0], before, SPAN)
    scalars = jnp.concatenate([y, starts.reshape(GROUP, ROWS)[:, 0] // ROWS])
    starts = starts.reshape(1, SPAN)

    done = [attend(c, scalars, starts, ordered[c], previous[c], arrived, [ordered[n] for n in LATER[c]])
            for c in chunks]
    returned = [shift_group(d[1], -1) for d in done]
    landed = []
    for n in range(len(OUT)):
        earlier = landed[AFTER[n]][1:] if AFTER[n] is not None else []
        landed.append(exchange(finish(n, y, done, returned, earlier)))
    outs = None
    for n in range(len(UNPACK)):
        outs = unpack(n, y, landed, outs)
    return tuple(outs)


def solution(mesh):
    rows = P(AXES, None)
    return jax.shard_map(
        shards,
        mesh=mesh,
        in_specs=(rows, rows, rows, rows, P(AXES)),
        out_specs=(rows, rows, rows, rows),
        check_vma=False,
    )
```
